128 devices in a mesh: owner: 32 (over x, z, core), loop: 4 (over y).
Axes of the slice: x: 4, y: 4, z: 4, core: 2. Of those that a mesh axis runs over, the one named last changes fastest.
Arguments:
- embeddings: bfloat16 [131072, 768], P(('owner', 'loop'))
- cluster_ids: int32 [131072], P(('owner', 'loop')), may hold values from 0 to 31, as said below
- row_order: int32 [131072], P(('owner', 'loop')), may hold values from 0 to 131071, each once
Outputs:
- best_similarity: float32 [131072], P(('owner', 'loop'))
The draws below stay inside these ranges and needn't reach their ends.
Inputs may be any that keep to these rules, and one draw needn't show every extreme that they name: `cluster_ids`: cluster c belongs to owner c. No device holds more than 64 rows of any one cluster, and one cluster, the same for every device, gets exactly 64 rows from each device.
All inputs are finite; a program needn't handle non-finite values.
Results may differ from the reference program's by a relative error of at most 0.00056.
Values may be sent and summed in bfloat16 or wider, within the bound.
A program may use at most 64 MiB of HBM per device.

```python
import math
import jax
import jax.numpy as jnp
from jax import lax

D = 768
ROWS = 1024
CAP = 64
CLUSTERS = 32
TOTAL = 131072
N_OWNER = 32
N_LOOP = 4


def spread_clusters(key):
    blocks = N_OWNER * N_LOOP
    slots = N_OWNER * CAP
    first, second, third, fourth = jax.random.split(key, 4)
    everyone = jax.random.randint(first, (), 0, N_OWNER)
    favored = jax.random.randint(second, (blocks, 1), 0, N_OWNER)
    slot_index = jnp.arange(slots, dtype=jnp.int32)[None, :]
    slot_owner = slot_index // CAP
    noise = jax.random.randint(third, (blocks, slots), 1, 2 ** 18)
    priority = (slot_owner == everyone) | (slot_owner == favored)
    score = jnp.where(priority, 0, noise) * slots + slot_index
    chosen = jnp.argsort(score, axis=1)[:, :ROWS]
    shuffle = jax.random.randint(fourth, (blocks, ROWS), 0, 2 ** 20) * ROWS + jnp.arange(ROWS, dtype=jnp.int32)[None, :]
    chosen = jnp.take_along_axis(chosen, jnp.argsort(shuffle, axis=1), axis=1)
    owner = chosen // CAP
    return owner.reshape(TOTAL).astype(jnp.int32)


def draw_cluster_ids(key, part):
    return spread_clusters(key)


def draw_embeddings(key, part):
    clusters = spread_clusters(key)
    key = jax.random.fold_in(key, 7)
    first, second, third = jax.random.split(key, 3)
    centers = jax.random.normal(first, (CLUSTERS, D), jnp.float32)
    strength = jnp.exp(jax.random.uniform(second, (TOTAL, 1), jnp.float32, math.log(0.2), math.log(2.0)))
    noise = jax.random.normal(third, (TOTAL, D), jnp.float32)
    values = strength * centers[clusters] + noise
    return values.astype(jnp.bfloat16)


def setup_inputs(seed: int = 0) -> dict:
    streams_of = jax.random.split(jax.random.key(seed), 4)
    embeddings = draw_embeddings(jax.random.fold_in(streams_of[3], 71), 0)
    cluster_ids = draw_cluster_ids(jax.random.fold_in(streams_of[3], 71), 0)
    row_order = jax.random.permutation(streams_of[2], TOTAL).astype(jnp.int32)
    return {"embeddings": embeddings, "cluster_ids": cluster_ids, "row_order": row_order}


epsilon = 1e-06

def normalize_rows(values):
    wide = values.astype(jnp.float32)
    scale = lax.rsqrt(lax.optimization_barrier(jnp.sum(wide * wide, axis=-1, keepdims=True)) + epsilon)
    return (wide * scale).astype(jnp.bfloat16)

def reference(embeddings, cluster_ids, row_order):
    total = embeddings.shape[0]
    unit = normalize_rows(embeddings)
    owner_of = cluster_ids
    keyed = owner_of * total + jnp.arange(total, dtype=jnp.int32)
    ranked = jnp.argsort(keyed).astype(jnp.int32)
    counts = lax.optimization_barrier(jnp.sum((owner_of[:, None] == jnp.arange(N_OWNER, dtype=jnp.int32)[None, :]).astype(jnp.int32), axis=0))
    starts = (jnp.cumsum(counts) - counts).astype(jnp.int32)
    span = N_OWNER * N_LOOP * CAP
    padded = jnp.concatenate([ranked, jnp.zeros((span,), jnp.int32)])

    def per_owner(owner):
        members = lax.dynamic_slice(padded, (starts[owner].astype(jnp.int32),), (span,))
        valid = jnp.arange(span, dtype=jnp.int32) < counts[owner]
        vectors = unit[members].astype(jnp.float32)
        clusters = jnp.where(valid, cluster_ids[members], -1)
        orders = row_order[members]
        scores = jnp.dot(vectors, vectors.T, precision=lax.Precision.HIGHEST)
        mask = (clusters[:, None] == clusters[None, :]) & (orders[None, :] < orders[:, None]) & valid[None, :]
        best = lax.optimization_barrier(jnp.max(jnp.where(mask, scores, -1.0), axis=1))
        target = jnp.where(valid, members, total)
        return (best, target)
    bests, targets = lax.map(per_owner, jnp.arange(N_OWNER, dtype=jnp.int32))
    result = jnp.full((total,), -1.0, jnp.float32)
    return result.at[targets.reshape(-1)].set(bests.reshape(-1), mode='drop')
```

```python
import functools

import jax
import jax.numpy as jnp
from jax import lax
from jax.experimental import pallas as pl
from jax.experimental.pallas import tpu as pltpu
from jax.sharding import PartitionSpec as P

MESH = pl.DeviceIdType.MESH
epsilon = 1e-06
D = 768
ROWS = 1024
CAP = 64
CHUNK = 256
STEPS = 8
CHUNKS = 32
FAR = float(2 ** 20)
WINDOW = 3

OFFSETS = [
    [(0, 0), (2, 2)], [(1, 0), (3, 0)], [(0, 1), (0, 3)], [(1, 1), (3, 3)],
    [(2, 1), (2, 3)], [(1, 3), (3, 1)], [(1, 2), (3, 2)], [(2, 0), (0, 2)],
]


def place(step):
    return step // 2 + 4 * (step % 2)


KEPT = ["q", "r", "p", "p", "q", "r", "p", "p"]
TO_0 = [step for step in range(STEPS) if KEPT[step] in "pq"]
TO_2 = [step for step in range(STEPS) if KEPT[step] in "pr"]
SIDE, THIRD, LATE_2, B0, LATE_0 = 8, 12, 16, 20, 28


def plan():
    tables = []
    for role in range(4):
        even = odd = 0
        side = third = low = high = late_low = late_high = 0
        steps = []
        for s in range(STEPS + 1):
            events = {}
            if s < STEPS:
                n = place(s)
                if role == 1:
                    if s % 2 == 0:
                        ranges = [(4, odd), (SIDE, high), (LATE_2, late_high)]
                    else:
                        ranges = [(0, even), (B0, low), (LATE_0, late_low)]
                    events["A"] = (n, ranges, False)
                else:
                    ranges = [(0, even), (4, odd)]
                    if role != 3:
                        ranges += [(SIDE, side), (THIRD, third)]
                    events["A"] = (n, ranges, True)
                if s % 2 == 0:
                    even += 1
                else:
                    odd += 1
            t = s - 1
            if t >= 0 and role in (0, 2):
                if t % 2 == (0 if role == 0 else 1):
                    events["B"] = (SIDE + side, [(0, even), (4, odd), (SIDE, side), (THIRD, third)], True)
                    side += 1
                if t in (TO_0 if role == 0 else TO_2):
                    events["C"] = (THIRD + third, [(0, even), (4, odd), (SIDE, side)], False)
                    third += 1
            if t >= 0 and role == 1:
                events["B"] = (SIDE + high, [(0, even), (B0, low), (LATE_0, late_low)], False)
                high += 1
                events["C"] = (B0 + low, [(4, odd), (SIDE, high), (LATE_2, late_high)], False)
                low += 1
                if s in (2, 6):
                    events["D"] = (LATE_0 + late_low, [(4, odd), (SIDE, high)], False)
                    late_low += 1
                if s in (3, 7):
                    events["D"] = (LATE_2 + late_high, [(0, even), (B0, low)], False)
                    late_high += 1
            steps.append(events)
        tables.append(steps)
    return tables


def kernel(emb, ids, order, out, unit, onehot, packed, rows, pos_rows, ord_rows, pos_col, ord_col,
           ord_out, ord_in, ord_lane, ord_sub, row_best, col_best, staged, shares, final, back,
           send_sem, recv_sem, osend_sem, orecv_sem, ysend_sem, yrecv_sem, yosend_sem, yorecv_sem,
           share_send, share_recv, back_send, back_recv):
    owner = lax.axis_index("owner")
    loop = lax.axis_index("loop")
    x, z, core = owner // 8, lax.rem(owner // 2, 4), lax.rem(owner, 2)
    role = jnp.where(core == 0, loop, lax.rem(loop + 2, 4))

    has_role = [(role == r).astype(jnp.int32) for r in range(4)]

    def device_of_role(r):
        return owner, lax.rem(r + 2 * core, 4)

    def by_role(values):
        if all(v == values[0] for v in values):
            return values[0]
        return sum(has_role[r] * values[r] for r in range(4) if values[r])

    def peers(step, sign):
        found = []
        for h, (dx, dz) in enumerate(OFFSETS[step]):
            for dc in range(2):
                slot = 4 * place(step) + 2 * h + dc
                if slot:
                    px = lax.rem(x + (dx if sign > 0 else 4 - dx), 4)
                    pz = lax.rem(z + (dz if sign > 0 else 4 - dz), 4)
                    pc = lax.rem(core + dc, 2)
                    found.append((slot, ((px * 4 + pz) * 2 + pc, loop)))
        return found

    barrier = pltpu.get_barrier_semaphore()
    for step in range(STEPS):
        for _, peer in peers(step, 1):
            pl.semaphore_signal(barrier, 1, device_id=peer, device_id_type=MESH)
    shares[...] = jnp.full(shares.shape, -1.0, jnp.float32)
    for d in (1, 2, 3):
        pl.semaphore_signal(barrier, 1, device_id=(owner, lax.rem(loop + d, 4)), device_id_type=MESH)

    cluster = ids[...]
    dx = (cluster // 8 - x + 4) % 4
    dz = (cluster // 2 % 4 - z + 4) % 4
    dc = (cluster - core + 2) % 2
    chip = dx * 4 + dz
    slot = jnp.zeros_like(cluster)
    for step in range(STEPS):
        for h, (ox, oz) in enumerate(OFFSETS[step]):
            slot = jnp.where(chip == ox * 4 + oz, 4 * place(step) + 2 * h, slot)
    slot = slot + dc
    slot_iota = lax.broadcasted_iota(jnp.int32, (32, 128), 0)
    hits = [(slot_iota == slot[j:j + 1, :]).astype(jnp.float32) for j in range(8)]
    earlier = (lax.broadcasted_iota(jnp.int32, (128, 128), 0)
               < lax.broadcasted_iota(jnp.int32, (128, 128), 1)).astype(jnp.bfloat16)
    before = jnp.zeros((32, 1), jnp.float32)
    for j in range(8):
        prefix = jnp.dot(hits[j].astype(jnp.bfloat16), earlier, preferred_element_type=jnp.float32)
        rank = jnp.sum(hits[j] * (prefix + before), axis=0, keepdims=True)
        before = before + jnp.sum(hits[j], axis=1, keepdims=True)
        pos = slot[j:j + 1, :].astype(jnp.float32) * CAP + rank
        pos_rows[j:j + 1, :] = pos
        pos_col[j * 128:(j + 1) * 128, :] = jnp.broadcast_to(pos, (128, 128)).T
        when = order[j:j + 1, :].astype(jnp.float32) - FAR
        ord_col[j * 128:(j + 1) * 128, :] = jnp.broadcast_to(when, (128, 128)).T

    def normalize(i, _):
        r = pl.ds(pl.multiple_of(i * 128, 128), 128)
        wide = emb[r, :].astype(jnp.float32)
        scale = lax.rsqrt(jnp.sum(wide * wide, axis=-1, keepdims=True) + epsilon)
        unit[r, :] = (wide * scale).astype(jnp.bfloat16)
        return 0

    lax.fori_loop(0, ROWS // 128, normalize, 0)

    def send(step, start):
        for s, peer in peers(step, 1):
            data = pltpu.make_async_remote_copy(
                src_ref=packed.at[pl.ds(s * CAP, CAP)], dst_ref=rows.at[pl.ds(s * CAP, CAP)],
                send_sem=send_sem.at[step], recv_sem=recv_sem.at[step], device_id=peer, device_id_type=MESH)
            data.start()
            when = pltpu.make_async_remote_copy(
                src_ref=ord_out.at[s // 2], dst_ref=ord_in.at[s],
                send_sem=osend_sem.at[step], recv_sem=orecv_sem.at[step], device_id=peer, device_id_type=MESH)
            when.start()

    def exchange_wait(step, sem, osem):
        skip = 1 if step == 0 else 0
        r = pl.ds(place(step) * CHUNK + skip * CAP, CHUNK - skip * CAP)
        pltpu.make_async_copy(packed.at[r], rows.at[r], sem.at[step]).wait()
        o = pl.ds(4 * place(step) + skip, 4 - skip)
        pltpu.make_async_copy(ord_in.at[o], ord_in.at[o], osem.at[step]).wait()

    lane = lax.broadcasted_iota(jnp.int32, (1024, 128), 1).astype(jnp.float32)
    for step in range(STEPS):
        first = place(step) * CHUNK
        wanted = lax.broadcasted_iota(jnp.int32, (CHUNK, 128), 0).astype(jnp.float32) + float(first)
        for j in range(8):
            onehot[:, j * 128:(j + 1) * 128] = (
                wanted == pos_rows[j:j + 1, :]).astype(jnp.float32).astype(jnp.bfloat16)
        block = jnp.dot(onehot[...], unit[...], preferred_element_type=jnp.float32).astype(jnp.bfloat16)
        packed[first:first + CHUNK, :] = block
        for pair in range(first // 128, first // 128 + 2):
            hit = pos_col[...] == lane + float(pair * 128)
            when = jnp.sum(jnp.where(hit, ord_col[...], 0.0), axis=0, keepdims=True) + FAR
            ord_out[pair] = jnp.broadcast_to(when, (8, 128))
        if step == 0:
            rows[0:CAP, :] = block[0:CAP, :]
            ord_in[0] = ord_out[0]
            pl.semaphore_wait(barrier, 34)
        if step < WINDOW:
            send(step, True)

    def clear(i, _):
        row_best[pl.ds(pl.multiple_of(i * CHUNK, CHUNK), CHUNK), :] = jnp.full((CHUNK, 128), -1.0, jnp.float32)
        col_best[pl.ds(2 * i, 2)] = jnp.full((2, 8, 128), -1.0, jnp.float32)
        return 0

    lax.fori_loop(0, CHUNKS, clear, 0)

    def spread(n):
        for h in range(2):
            when = jnp.broadcast_to(ord_lane[2 * n + h][0:1, :], (128, 128))
            at = n * CHUNK + h * 128
            ord_sub[pl.ds(at if isinstance(at, int) else pl.multiple_of(at, 128), 128), :] = when.T

    def rows_of(n):
        at = n * CHUNK
        return pl.ds(at if isinstance(at, int) else pl.multiple_of(at, CHUNK), CHUNK)

    def scores(m, n):
        return lax.dot_general(rows[rows_of(m), :], rows[rows_of(n), :], (((1,), (1,)), ((), ())),
                               preferred_element_type=jnp.float32)

    def cross(m, n):
        s = scores(m, n)
        mine = ord_sub[rows_of(m), :]
        best = row_best[rows_of(m), :]
        for h in range(2):
            part = s[:, h * 128:(h + 1) * 128]
            mask = ord_lane[2 * n + h][0:1, :] < mine
            best = jnp.maximum(best, jnp.where(mask, part, -1.0))
            other = jnp.where(mask, -1.0, part).reshape(CHUNK // 8, 8, 128)
            col_best[2 * n + h] = jnp.maximum(col_best[2 * n + h], jnp.max(other, axis=0))
        row_best[rows_of(m), :] = best

    def alone(n):
        s = scores(n, n)
        mine = ord_sub[rows_of(n), :]
        best = row_best[rows_of(n), :]
        for h in range(2):
            mask = ord_lane[2 * n + h][0:1, :] < mine
            best = jnp.maximum(best, jnp.where(mask, s[:, h * 128:(h + 1) * 128], -1.0))
        row_best[rows_of(n), :] = best

    tables = plan()

    def meet(s, name):
        events = [tables[r][s].get(name) for r in range(4)]
        n = by_role([e[0] if e else 0 for e in events])
        depth = max(len(e[1]) for e in events if e)
        starts, counts = [], []
        for k in range(depth):
            ranges = [e[1][k] if e and k < len(e[1]) else (0, 0) for e in events]
            starts.append(by_role([r[0] for r in ranges]))
            counts.append(by_role([r[1] for r in ranges]))
        total = by_role([sum(r[1] for r in e[1]) if e else 0 for e in events])

        def body(t, _):
            m = t + starts[0]
            passed = counts[0]
            for k in range(1, depth):
                m = jnp.where(t >= passed, t - passed + starts[k], m)
                passed = passed + counts[k]
            cross(m, n)
            return 0

        if any(sum(r[1] for r in e[1]) for e in events if e):
            lax.fori_loop(0, total, body, 0)
        selves = [1 if e and e[2] else 0 for e in events]
        if any(selves):
            @pl.when(by_role(selves) == 1)
            def _():
                alone(n)

    def share_rows(src, dst, to, send_index, recv_index):
        data = pltpu.make_async_remote_copy(
            src_ref=rows.at[rows_of(src)], dst_ref=rows.at[rows_of(dst)],
            send_sem=ysend_sem.at[send_index], recv_sem=yrecv_sem.at[recv_index],
            device_id=device_of_role(to), device_id_type=MESH)
        when = pltpu.make_async_remote_copy(
            src_ref=ord_lane.at[pl.ds(2 * src, 2)], dst_ref=ord_lane.at[pl.ds(2 * dst, 2)],
            send_sem=yosend_sem.at[send_index], recv_sem=yorecv_sem.at[recv_index],
            device_id=device_of_role(to), device_id_type=MESH)
        return data, when

    sends = [[], [], [], []]

    def forward(r, src, dst, to):
        @pl.when(role == r)
        def _():
            index = len(sends[r])
            for copy in share_rows(src, dst, to, index, dst - 8):
                copy.start()
            sends[r].append((src, dst, to))

    def arrive(s, name):
        events = [tables[r][s].get(name) for r in range(4)]
        for r in range(4):
            if not events[r]:
                continue

            @pl.when(role == r)
            def _():
                n = events[r][0]
                for copy in share_rows(n, n, (r + 1) % 4, 0, n - 8):
                    copy.wait_recv()
                if r in (0, 2) and name == "C" and n in (THIRD, THIRD + 3):
                    index = len(sends[r])
                    late = LATE_0 if r == 0 else LATE_2
                    late = late + (n - THIRD) // 3
                    for copy in share_rows(n, late, 1, index, late - 8):
                        copy.start()
                    sends[r].append((n, late, 1))
                spread(n)

    low_half = lax.broadcasted_iota(jnp.int32, (8, 128), 1) < CAP
    for s in range(STEPS + 1):
        if s < STEPS:
            n = place(s)
            exchange_wait(s, send_sem, osend_sem)
            if s + WINDOW < STEPS:
                send(s + WINDOW, True)
            exchange_wait(s, recv_sem, orecv_sem)
            for h in range(2):
                ord_lane[2 * n + h] = jnp.where(low_half, ord_in[4 * n + 2 * h], ord_in[4 * n + 2 * h + 1])
            forward(0, n, B0 + s, 1)
            forward(2, n, SIDE + s, 1)
            forward(1, n, SIDE + s // 2, 0 if s % 2 == 0 else 2)
            if KEPT[s] in "pq":
                forward(3, n, THIRD + TO_0.index(s), 0)
            if KEPT[s] in "pr":
                forward(3, n, THIRD + TO_2.index(s), 2)
            spread(n)
            meet(s, "A")
        for names in ("BC", "D"):
            present = [name for name in names if any(tables[r][s].get(name) for r in range(4))]
            for name in present:
                arrive(s, name)
            for name in present:
                meet(s, name)

    def line(i):
        turned = row_best[i * 128:(i + 1) * 128, :].T
        return jnp.maximum(jnp.max(turned, axis=0, keepdims=True), jnp.max(col_best[i], axis=0, keepdims=True))

    def give(r, groups):
        @pl.when(role == r)
        def _():
            copies = []
            for to, pairs in groups:
                used = {place(step): n for n, step in pairs}
                for p in range(STEPS):
                    for h in range(2):
                        i = 2 * p + h
                        value = line(2 * used[p] + h) if p in used else jnp.full((1, 128), -1.0, jnp.float32)
                        staged[to, i // 8, i % 8:i % 8 + 1, :] = value
                copies.append(pltpu.make_async_remote_copy(
                    src_ref=staged.at[to], dst_ref=shares.at[r], send_sem=share_send.at[to],
                    recv_sem=share_recv.at[r], device_id=device_of_role(to), device_id_type=MESH))
                copies[-1].start()
            for copy in copies:
                copy.wait_send()

    give(0, [(3, [(THIRD + k, t) for k, t in enumerate(TO_0)]), (1, [(SIDE + k, 2 * k) for k in range(4)])])
    give(2, [(3, [(THIRD + k, t) for k, t in enumerate(TO_2)]), (1, [(SIDE + k, 2 * k + 1) for k in range(4)])])
    give(1, [(3, [(LATE_0, 0), (LATE_0 + 1, 4), (LATE_2, 1), (LATE_2 + 1, 5)]),
             (0, [(B0 + k, k) for k in range(8)]), (2, [(SIDE + k, k) for k in range(8)])])
    for r, givers in enumerate(((1,), (0, 2), (1,), (0, 1, 2))):
        @pl.when(role == r)
        def _():
            for giver in givers:
                pltpu.make_async_remote_copy(
                    src_ref=staged.at[0], dst_ref=shares.at[giver], send_sem=share_send.at[0],
                    recv_sem=share_recv.at[giver], device_id=device_of_role(giver),
                    device_id_type=MESH).wait_recv()

    for i in range(16):
        value = line(i)
        for r in range(3):
            value = jnp.maximum(value, shares[r, i // 8, i % 8:i % 8 + 1, :])
        final[i] = jnp.broadcast_to(value, (8, 128))
    back[0] = final[0]
    for step in range(STEPS):
        for s, peer in peers(step, -1):
            pltpu.make_async_remote_copy(
                src_ref=final.at[s // 2], dst_ref=back.at[s], send_sem=back_send.at[0],
                recv_sem=back_recv.at[0], device_id=peer, device_id_type=MESH).start()
    pltpu.make_async_copy(back.at[pl.ds(1, 31)], back.at[pl.ds(1, 31)], back_recv.at[0]).wait()
    for i in range(16):
        final_line = jnp.where(low_half, back[2 * i], back[2 * i + 1])
        ord_in[i] = final_line

    def collect(j, _):
        at = pos_col[pl.ds(pl.multiple_of(j * 128, 128), 128), :]
        found = jnp.zeros((128, 128), jnp.float32)
        spot = lane[0:128, :]
        for i in range(16):
            found = jnp.where(at == spot + float(i * 128), ord_in[i][0:1, :], found)
        out[pl.ds(j, 1), :] = jnp.sum(found.T, axis=0, keepdims=True)
        return 0

    lax.fori_loop(0, 8, collect, 0)
    pltpu.make_async_copy(back.at[pl.ds(1, 31)], back.at[pl.ds(1, 31)], back_send.at[0]).wait()
    for r in range(4):
        @pl.when(role == r)
        def _():
            for index, (src, dst, to) in enumerate(sends[r]):
                for copy in share_rows(src, dst, to, index, dst - 8):
                    copy.wait_send()


def on_device(embeddings, cluster_ids, row_order):
    best = pl.pallas_call(
        kernel,
        out_shape=jax.ShapeDtypeStruct((8, 128), jnp.float32),
        in_specs=[pl.BlockSpec(memory_space=pltpu.VMEM)] * 3,
        out_specs=pl.BlockSpec(memory_space=pltpu.VMEM),
        scratch_shapes=[
            pltpu.VMEM((ROWS, D), jnp.bfloat16),
            pltpu.VMEM((CHUNK, ROWS), jnp.bfloat16),
            pltpu.VMEM((STEPS * CHUNK, D), jnp.bfloat16),
            pltpu.VMEM((CHUNKS * CHUNK, D), jnp.bfloat16),
            pltpu.VMEM((8, 128), jnp.float32),
            pltpu.VMEM((8, 128), jnp.float32),
            pltpu.VMEM((ROWS, 128), jnp.float32),
            pltpu.VMEM((ROWS, 128), jnp.float32),
            pltpu.VMEM((16, 8, 128), jnp.float32),
            pltpu.VMEM((32, 8, 128), jnp.float32),
            pltpu.VMEM((2 * CHUNKS, 8, 128), jnp.float32),
            pltpu.VMEM((CHUNKS * CHUNK, 128), jnp.float32),
            pltpu.VMEM((CHUNKS * CHUNK, 128), jnp.float32),
            pltpu.VMEM((2 * CHUNKS, 8, 128), jnp.float32),
            pltpu.VMEM((4, 2, 8, 128), jnp.float32),
            pltpu.VMEM((4, 2, 8, 128), jnp.float32),
            pltpu.VMEM((16, 8, 128), jnp.float32),
            pltpu.VMEM((32, 8, 128), jnp.float32),
            pltpu.SemaphoreType.DMA((STEPS,)),
            pltpu.SemaphoreType.DMA((STEPS,)),
            pltpu.SemaphoreType.DMA((STEPS,)),
            pltpu.SemaphoreType.DMA((STEPS,)),
            pltpu.SemaphoreType.DMA((16,)),
            pltpu.SemaphoreType.DMA((24,)),
            pltpu.SemaphoreType.DMA((16,)),
            pltpu.SemaphoreType.DMA((24,)),
            pltpu.SemaphoreType.DMA((4,)),
            pltpu.SemaphoreType.DMA((4,)),
            pltpu.SemaphoreType.DMA((1,)),
            pltpu.SemaphoreType.DMA((1,)),
        ],
        compiler_params=pltpu.CompilerParams(
            collective_id=0, has_side_effects=True, vmem_limit_bytes=56 * 1024 * 1024),
        name="best_match",
    )(embeddings, cluster_ids.reshape(8, 128), row_order.reshape(8, 128))
    return best.reshape(ROWS)


def solution(mesh):
    return jax.shard_map(
        on_device,
        mesh=mesh,
        in_specs=(P(("owner", "loop"), None), P(("owner", "loop")), P(("owner", "loop"))),
        out_specs=P(("owner", "loop")),
        check_vma=False,
    )
```

```python
import functools

import jax
import jax.numpy as jnp
from jax import lax
from jax.experimental import pallas as pl
from jax.experimental.pallas import tpu as pltpu
from jax.sharding import PartitionSpec as P

MESH = pl.DeviceIdType.MESH
epsilon = 1e-06
D = 768
ROWS = 1024
CAP = 64
CHUNK = 256
STEPS = 8
CHUNKS = 32
FAR = float(2 ** 20)
WINDOW = 3
GROUP = 4

OFFSETS = [
    [(0, 0), (2, 2)], [(1, 0), (3, 0)], [(0, 1), (0, 3)], [(1, 1), (3, 3)],
    [(2, 1), (2, 3)], [(1, 3), (3, 1)], [(1, 2), (3, 2)], [(2, 0), (0, 2)],
]


def place(step):
    return step // 2 + 4 * (step % 2)


KEPT = ["q", "r", "p", "p", "q", "r", "p", "p"]
TO_0 = [step for step in range(STEPS) if KEPT[step] in "pq"]
TO_2 = [step for step in range(STEPS) if KEPT[step] in "pr"]
SIDE, THIRD, LATE_2, B0, LATE_0 = 8, 12, 16, 20, 28


def plan():
    tables = []
    for role in range(4):
        even = odd = 0
        side = third = low = high = late_low = late_high = 0
        steps = []
        for s in range(STEPS + 1):
            events = {}
            if s < STEPS:
                n = place(s)
                if role == 1:
                    if s % 2 == 0:
                        ranges = [(4, odd), (SIDE, high), (LATE_2, late_high)]
                    else:
                        ranges = [(0, even), (B0, low), (LATE_0, late_low)]
                    events["A"] = (n, ranges, False)
                else:
                    ranges = [(0, even), (4, odd)]
                    if role != 3:
                        ranges += [(SIDE, side), (THIRD, third)]
                    events["A"] = (n, ranges, True)
                if s % 2 == 0:
                    even += 1
                else:
                    odd += 1
            t = s - 1
            if t >= 0 and role in (0, 2):
                if t % 2 == (0 if role == 0 else 1):
                    events["B"] = (SIDE + side, [(0, even), (4, odd), (SIDE, side), (THIRD, third)], True)
                    side += 1
                if t in (TO_0 if role == 0 else TO_2):
                    events["C"] = (THIRD + third, [(0, even), (4, odd), (SIDE, side)], False)
                    third += 1
            if t >= 0 and role == 1:
                events["B"] = (SIDE + high, [(0, even), (B0, low), (LATE_0, late_low)], False)
                high += 1
                events["C"] = (B0 + low, [(4, odd), (SIDE, high), (LATE_2, late_high)], False)
                low += 1
                if s in (2, 6):
                    events["D"] = (LATE_0 + late_low, [(4, odd), (SIDE, high)], False)
                    late_low += 1
                if s in (3, 7):
                    events["D"] = (LATE_2 + late_high, [(0, even), (B0, low)], False)
                    late_high += 1
            steps.append(events)
        tables.append(steps)
    return tables


def kernel(emb, ids, order, out, unit, onehot, packed, rows, pos_rows, ord_rows, pos_col, ord_col,
           ord_out, ord_in, ord_lane, ord_sub, row_best, col_best, staged, shares, final, back,
           send_sem, recv_sem, osend_sem, orecv_sem, ysend_sem, yrecv_sem, yosend_sem, yorecv_sem,
           share_send, share_recv, back_send, back_recv):
    owner = lax.axis_index("owner")
    loop = lax.axis_index("loop")
    x, z, core = owner // 8, lax.rem(owner // 2, 4), lax.rem(owner, 2)
    role = jnp.where(core == 0, loop, lax.rem(loop + 2, 4))

    has_role = [(role == r).astype(jnp.int32) for r in range(4)]

    def device_of_role(r):
        return owner, lax.rem(r + 2 * core, 4)

    def by_role(values):
        if all(v == values[0] for v in values):
            return values[0]
        return sum(has_role[r] * values[r] for r in range(4) if values[r])

    def peers(step, sign):
        found = []
        for h, (dx, dz) in enumerate(OFFSETS[step]):
            for dc in range(2):
                slot = 4 * place(step) + 2 * h + dc
                if slot:
                    px = lax.rem(x + (dx if sign > 0 else 4 - dx), 4)
                    pz = lax.rem(z + (dz if sign > 0 else 4 - dz), 4)
                    pc = lax.rem(core + dc, 2)
                    found.append((slot, ((px * 4 + pz) * 2 + pc, loop)))
        return found

    barrier = pltpu.get_barrier_semaphore()
    for step in range(STEPS):
        for _, peer in peers(step, 1):
            pl.semaphore_signal(barrier, 1, device_id=peer, device_id_type=MESH)
    shares[...] = jnp.full(shares.shape, -1.0, jnp.float32)
    for d in (1, 2, 3):
        pl.semaphore_signal(barrier, 1, device_id=(owner, lax.rem(loop + d, 4)), device_id_type=MESH)

    cluster = ids[...]
    dx = (cluster // 8 - x + 4) % 4
    dz = (cluster // 2 % 4 - z + 4) % 4
    dc = (cluster - core + 2) % 2
    chip = dx * 4 + dz
    slot = jnp.zeros_like(cluster)
    for step in range(STEPS):
        for h, (ox, oz) in enumerate(OFFSETS[step]):
            slot = jnp.where(chip == ox * 4 + oz, 4 * place(step) + 2 * h, slot)
    slot = slot + dc
    slot_iota = lax.broadcasted_iota(jnp.int32, (32, 128), 0)
    hits = [(slot_iota == slot[j:j + 1, :]).astype(jnp.float32) for j in range(8)]
    earlier = (lax.broadcasted_iota(jnp.int32, (128, 128), 0)
               < lax.broadcasted_iota(jnp.int32, (128, 128), 1)).astype(jnp.bfloat16)
    before = jnp.zeros((32, 1), jnp.float32)
    for j in range(8):
        prefix = jnp.dot(hits[j].astype(jnp.bfloat16), earlier, preferred_element_type=jnp.float32)
        rank = jnp.sum(hits[j] * (prefix + before), axis=0, keepdims=True)
        before = before + jnp.sum(hits[j], axis=1, keepdims=True)
        pos = slot[j:j + 1, :].astype(jnp.float32) * CAP + rank
        pos_rows[j:j + 1, :] = pos
        pos_col[j * 128:(j + 1) * 128, :] = jnp.broadcast_to(pos, (128, 128)).T
        when = order[j:j + 1, :].astype(jnp.float32) - FAR
        ord_col[j * 128:(j + 1) * 128, :] = jnp.broadcast_to(when, (128, 128)).T

    def normalize(i, _):
        r = pl.ds(pl.multiple_of(i * 128, 128), 128)
        wide = emb[r, :].astype(jnp.float32)
        scale = lax.rsqrt(jnp.sum(wide * wide, axis=-1, keepdims=True) + epsilon)
        unit[r, :] = (wide * scale).astype(jnp.bfloat16)
        return 0

    lax.fori_loop(0, ROWS // 128, normalize, 0)

    def send(step, start):
        for s, peer in peers(step, 1):
            data = pltpu.make_async_remote_copy(
                src_ref=packed.at[pl.ds(s * CAP, CAP)], dst_ref=rows.at[pl.ds(s * CAP, CAP)],
                send_sem=send_sem.at[step], recv_sem=recv_sem.at[step], device_id=peer, device_id_type=MESH)
            data.start()
            when = pltpu.make_async_remote_copy(
                src_ref=ord_out.at[s // 2], dst_ref=ord_in.at[s],
                send_sem=osend_sem.at[step], recv_sem=orecv_sem.at[step], device_id=peer, device_id_type=MESH)
            when.start()

    def exchange_wait(step, sem, osem):
        skip = 1 if step == 0 else 0
        r = pl.ds(place(step) * CHUNK + skip * CAP, CHUNK - skip * CAP)
        pltpu.make_async_copy(packed.at[r], rows.at[r], sem.at[step]).wait()
        o = pl.ds(4 * place(step) + skip, 4 - skip)
        pltpu.make_async_copy(ord_in.at[o], ord_in.at[o], osem.at[step]).wait()

    lane = lax.broadcasted_iota(jnp.int32, (1024, 128), 1).astype(jnp.float32)
    for step in range(STEPS):
        first = place(step) * CHUNK
        wanted = lax.broadcasted_iota(jnp.int32, (CHUNK, 128), 0).astype(jnp.float32) + float(first)
        for j in range(8):
            onehot[:, j * 128:(j + 1) * 128] = (
                wanted == pos_rows[j:j + 1, :]).astype(jnp.float32).astype(jnp.bfloat16)
        block = jnp.dot(onehot[...], unit[...], preferred_element_type=jnp.float32).astype(jnp.bfloat16)
        packed[first:first + CHUNK, :] = block
        for pair in range(first // 128, first // 128 + 2):
            hit = pos_col[...] == lane + float(pair * 128)
            when = jnp.sum(jnp.where(hit, ord_col[...], 0.0), axis=0, keepdims=True) + FAR
            ord_out[pair] = jnp.broadcast_to(when, (8, 128))
        if step == 0:
            rows[0:CAP, :] = block[0:CAP, :]
            ord_in[0] = ord_out[0]
            pl.semaphore_wait(barrier, 34)
        if step < WINDOW:
            send(step, True)

    def clear(i, _):
        row_best[pl.ds(pl.multiple_of(i * CHUNK, CHUNK), CHUNK), :] = jnp.full((CHUNK, 128), -1.0, jnp.float32)
        col_best[pl.ds(2 * i, 2)] = jnp.full((2, 8, 128), -1.0, jnp.float32)
        return 0

    lax.fori_loop(0, CHUNKS, clear, 0)

    def spread(n):
        for h in range(2):
            when = jnp.broadcast_to(ord_lane[2 * n + h][0:1, :], (128, 128))
            at = n * CHUNK + h * 128
            ord_sub[pl.ds(at if isinstance(at, int) else pl.multiple_of(at, 128), 128), :] = when.T

    def rows_of(n):
        at = n * CHUNK
        return pl.ds(at if isinstance(at, int) else pl.multiple_of(at, CHUNK), CHUNK)

    def cross(ms, n):
        held = jnp.concatenate([rows[rows_of(m), :] for m in ms], axis=0)
        s = lax.dot_general(held, rows[rows_of(n), :], (((1,), (1,)), ((), ())), preferred_element_type=jnp.float32)
        for k, m in enumerate(ms):
            mine = ord_sub[rows_of(m), :]
            best = row_best[rows_of(m), :]
            for h in range(2):
                part = s[k * CHUNK:(k + 1) * CHUNK, h * 128:(h + 1) * 128]
                when = ord_lane[2 * n + h][0:1, :]
                best = jnp.maximum(best, jnp.where(when < mine, part, -1.0))
                other = jnp.where(mine < when, part, -1.0).reshape(CHUNK // 8, 8, 128)
                col_best[2 * n + h] = jnp.maximum(col_best[2 * n + h], jnp.max(other, axis=0))
            row_best[rows_of(m), :] = best

    tables = plan()

    def meet(s, name):
        events = [tables[r][s].get(name) for r in range(4)]
        n = by_role([e[0] if e else 0 for e in events])
        lists = [[r for r in e[1] if r[1]] + ([(e[0], 1)] if e[2] else []) if e else [] for e in events]
        depth = max(len(ranges) for ranges in lists)
        if not depth:
            return
        starts, counts = [], []
        for k in range(depth):
            ranges = [ranges[k] if k < len(ranges) else (0, 0) for ranges in lists]
            starts.append(by_role([r[0] for r in ranges]))
            counts.append(by_role([r[1] for r in ranges]))
        total = by_role([sum(r[1] for r in ranges) for ranges in lists])

        def member(t):
            t = jnp.minimum(t, total - 1)
            m = t + starts[0]
            passed = counts[0]
            for k in range(1, depth):
                m = jnp.where(t >= passed, t - passed + starts[k], m)
                passed = passed + counts[k]
            return m

        def body(t, _):
            cross([member(t * GROUP + k) for k in range(GROUP)], n)
            return 0

        lax.fori_loop(0, (total + GROUP - 1) // GROUP, body, 0)

    def share_rows(src, dst, to, send_index, recv_index):
        data = pltpu.make_async_remote_copy(
            src_ref=rows.at[rows_of(src)], dst_ref=rows.at[rows_of(dst)],
            send_sem=ysend_sem.at[send_index], recv_sem=yrecv_sem.at[recv_index],
            device_id=device_of_role(to), device_id_type=MESH)
        when = pltpu.make_async_remote_copy(
            src_ref=ord_lane.at[pl.ds(2 * src, 2)], dst_ref=ord_lane.at[pl.ds(2 * dst, 2)],
            send_sem=yosend_sem.at[send_index], recv_sem=yorecv_sem.at[recv_index],
            device_id=device_of_role(to), device_id_type=MESH)
        return data, when

    sends = [[], [], [], []]

    def forward(r, src, dst, to):
        @pl.when(role == r)
        def _():
            index = len(sends[r])
            for copy in share_rows(src, dst, to, index, dst - 8):
                copy.start()
            sends[r].append((src, dst, to))

    def arrive(s, name):
        events = [tables[r][s].get(name) for r in range(4)]
        for r in range(4):
            if not events[r]:
                continue

            @pl.when(role == r)
            def _():
                n = events[r][0]
                for copy in share_rows(n, n, (r + 1) % 4, 0, n - 8):
                    copy.wait_recv()
                if r in (0, 2) and name == "C" and n in (THIRD, THIRD + 3):
                    index = len(sends[r])
                    late = LATE_0 if r == 0 else LATE_2
                    late = late + (n - THIRD) // 3
                    for copy in share_rows(n, late, 1, index, late - 8):
                        copy.start()
                    sends[r].append((n, late, 1))
                spread(n)

    low_half = lax.broadcasted_iota(jnp.int32, (8, 128), 1) < CAP
    for s in range(STEPS + 1):
        if s < STEPS:
            n = place(s)
            exchange_wait(s, send_sem, osend_sem)
            if s + WINDOW < STEPS:
                send(s + WINDOW, True)
            exchange_wait(s, recv_sem, orecv_sem)
            for h in range(2):
                ord_lane[2 * n + h] = jnp.where(low_half, ord_in[4 * n + 2 * h], ord_in[4 * n + 2 * h + 1])
            forward(0, n, B0 + s, 1)
            forward(2, n, SIDE + s, 1)
            forward(1, n, SIDE + s // 2, 0 if s % 2 == 0 else 2)
            if KEPT[s] in "pq":
                forward(3, n, THIRD + TO_0.index(s), 0)
            if KEPT[s] in "pr":
                forward(3, n, THIRD + TO_2.index(s), 2)
            spread(n)
            meet(s, "A")
        for names in ("BC", "D"):
            present = [name for name in names if any(tables[r][s].get(name) for r in range(4))]
            for name in present:
                arrive(s, name)
            for name in present:
                meet(s, name)

    def line(i):
        turned = row_best[i * 128:(i + 1) * 128, :].T
        return jnp.maximum(jnp.max(turned, axis=0, keepdims=True), jnp.max(col_best[i], axis=0, keepdims=True))

    def give(r, groups):
        @pl.when(role == r)
        def _():
            copies = []
            for to, pairs in groups:
                used = {place(step): n for n, step in pairs}
                for p in range(STEPS):
                    for h in range(2):
                        i = 2 * p + h
                        value = line(2 * used[p] + h) if p in used else jnp.full((1, 128), -1.0, jnp.float32)
                        staged[to, i // 8, i % 8:i % 8 + 1, :] = value
                copies.append(pltpu.make_async_remote_copy(
                    src_ref=staged.at[to], dst_ref=shares.at[r], send_sem=share_send.at[to],
                    recv_sem=share_recv.at[r], device_id=device_of_role(to), device_id_type=MESH))
                copies[-1].start()
            for copy in copies:
                copy.wait_send()

    give(0, [(3, [(THIRD + k, t) for k, t in enumerate(TO_0)]), (1, [(SIDE + k, 2 * k) for k in range(4)])])
    give(2, [(3, [(THIRD + k, t) for k, t in enumerate(TO_2)]), (1, [(SIDE + k, 2 * k + 1) for k in range(4)])])
    give(1, [(3, [(LATE_0, 0), (LATE_0 + 1, 4), (LATE_2, 1), (LATE_2 + 1, 5)]),
             (0, [(B0 + k, k) for k in range(8)]), (2, [(SIDE + k, k) for k in range(8)])])
    for r, givers in enumerate(((1,), (0, 2), (1,), (0, 1, 2))):
        @pl.when(role == r)
        def _():
            for giver in givers:
                pltpu.make_async_remote_copy(
                    src_ref=staged.at[0], dst_ref=shares.at[giver], send_sem=share_send.at[0],
                    recv_sem=share_recv.at[giver], device_id=device_of_role(giver),
                    device_id_type=MESH).wait_recv()

    for i in range(16):
        value = line(i)
        for r in range(3):
            value = jnp.maximum(value, shares[r, i // 8, i % 8:i % 8 + 1, :])
        final[i] = jnp.broadcast_to(value, (8, 128))
    back[0] = final[0]
    for step in range(STEPS):
        for s, peer in peers(step, -1):
            pltpu.make_async_remote_copy(
                src_ref=final.at[s // 2], dst_ref=back.at[s], send_sem=back_send.at[0],
                recv_sem=back_recv.at[0], device_id=peer, device_id_type=MESH).start()
    pltpu.make_async_copy(back.at[pl.ds(1, 31)], back.at[pl.ds(1, 31)], back_recv.at[0]).wait()
    for i in range(16):
        final_line = jnp.where(low_half, back[2 * i], back[2 * i + 1])
        ord_in[i] = final_line

    def collect(j, _):
        at = pos_col[pl.ds(pl.multiple_of(j * 128, 128), 128), :]
        found = jnp.zeros((128, 128), jnp.float32)
        spot = lane[0:128, :]
        for i in range(16):
            found = jnp.where(at == spot + float(i * 128), ord_in[i][0:1, :], found)
        out[pl.ds(j, 1), :] = jnp.sum(found.T, axis=0, keepdims=True)
        return 0

    lax.fori_loop(0, 8, collect, 0)
    pltpu.make_async_copy(back.at[pl.ds(1, 31)], back.at[pl.ds(1, 31)], back_send.at[0]).wait()
    for r in range(4):
        @pl.when(role == r)
        def _():
            for index, (src, dst, to) in enumerate(sends[r]):
                for copy in share_rows(src, dst, to, index, dst - 8):
                    copy.wait_send()


def on_device(embeddings, cluster_ids, row_order):
    best = pl.pallas_call(
        kernel,
        out_shape=jax.ShapeDtypeStruct((8, 128), jnp.float32),
        in_specs=[pl.BlockSpec(memory_space=pltpu.VMEM)] * 3,
        out_specs=pl.BlockSpec(memory_space=pltpu.VMEM),
        scratch_shapes=[
            pltpu.VMEM((ROWS, D), jnp.bfloat16),
            pltpu.VMEM((CHUNK, ROWS), jnp.bfloat16),
            pltpu.VMEM((STEPS * CHUNK, D), jnp.bfloat16),
            pltpu.VMEM((CHUNKS * CHUNK, D), jnp.bfloat16),
            pltpu.VMEM((8, 128), jnp.float32),
            pltpu.VMEM((8, 128), jnp.float32),
            pltpu.VMEM((ROWS, 128), jnp.float32),
            pltpu.VMEM((ROWS, 128), jnp.float32),
            pltpu.VMEM((16, 8, 128), jnp.float32),
            pltpu.VMEM((32, 8, 128), jnp.float32),
            pltpu.VMEM((2 * CHUNKS, 8, 128), jnp.float32),
            pltpu.VMEM((CHUNKS * CHUNK, 128), jnp.float32),
            pltpu.VMEM((CHUNKS * CHUNK, 128), jnp.float32),
            pltpu.VMEM((2 * CHUNKS, 8, 128), jnp.float32),
            pltpu.VMEM((4, 2, 8, 128), jnp.float32),
            pltpu.VMEM((4, 2, 8, 128), jnp.float32),
            pltpu.VMEM((16, 8, 128), jnp.float32),
            pltpu.VMEM((32, 8, 128), jnp.float32),
            pltpu.SemaphoreType.DMA((STEPS,)),
            pltpu.SemaphoreType.DMA((STEPS,)),
            pltpu.SemaphoreType.DMA((STEPS,)),
            pltpu.SemaphoreType.DMA((STEPS,)),
            pltpu.SemaphoreType.DMA((16,)),
            pltpu.SemaphoreType.DMA((24,)),
            pltpu.SemaphoreType.DMA((16,)),
            pltpu.SemaphoreType.DMA((24,)),
            pltpu.SemaphoreType.DMA((4,)),
            pltpu.SemaphoreType.DMA((4,)),
            pltpu.SemaphoreType.DMA((1,)),
            pltpu.SemaphoreType.DMA((1,)),
        ],
        compiler_params=pltpu.CompilerParams(
            collective_id=0, has_side_effects=True, vmem_limit_bytes=56 * 1024 * 1024),
        name="best_match",
    )(embeddings, cluster_ids.reshape(8, 128), row_order.reshape(8, 128))
    return best.reshape(ROWS)


def solution(mesh):
    return jax.shard_map(
        on_device,
        mesh=mesh,
        in_specs=(P(("owner", "loop"), None), P(("owner", "loop")), P(("owner", "loop"))),
        out_specs=P(("owner", "loop")),
        check_vma=False,
    )
```

```python
import functools

import jax
import jax.numpy as jnp
from jax import lax
from jax.experimental import pallas as pl
from jax.experimental.pallas import tpu as pltpu
from jax.sharding import PartitionSpec as P

MESH = pl.DeviceIdType.MESH
epsilon = 1e-06
D = 768
ROWS = 1024
CAP = 64
CHUNK = 256
STEPS = 8
CHUNKS = 32
FAR = float(2 ** 20)
WINDOW = 3
WIDEST = 8


def width(totals):
    def cost(group):
        return max(-(-total // group) for total in totals) * (2.3 + group)

    return min(range(1, WIDEST + 1), key=cost)


OFFSETS = [
    [(0, 0), (2, 2)], [(1, 0), (3, 0)], [(0, 1), (0, 3)], [(1, 1), (3, 3)],
    [(2, 1), (2, 3)], [(1, 3), (3, 1)], [(1, 2), (3, 2)], [(2, 0), (0, 2)],
]
FAR_FIRST = (0, 4, 6, 3, 5, 7, 1, 2)


def place(step):
    return step // 2 + 4 * (step % 2)


KEPT = ["q", "r", "p", "p", "q", "r", "p", "p"]
RELAY_0 = [step for step in range(STEPS) if KEPT[step] == "q"]
RELAY_2 = [step for step in range(STEPS) if KEPT[step] == "r"]
TO_0 = [step for step in range(STEPS) if KEPT[step] in "pq"]
TO_2 = [step for step in range(STEPS) if KEPT[step] in "pr"]
SIDE, THIRD, LATE_2, B0, LATE_0 = 8, 12, 16, 20, 28


def plan():
    tables = []
    for role in range(4):
        even = odd = 0
        side = third = low = high = late_low = late_high = 0
        steps = []
        for s in range(STEPS + 1):
            events = {}
            if s < STEPS:
                n = place(s)
                if role == 1:
                    if s % 2 == 0:
                        ranges = [(4, odd), (SIDE, high), (LATE_2, late_high)]
                    else:
                        ranges = [(0, even), (B0, low), (LATE_0, late_low)]
                    events["A"] = (n, ranges, False)
                else:
                    ranges = [(0, even), (4, odd)]
                    if role != 3:
                        ranges += [(SIDE, side), (THIRD, third)]
                    events["A"] = (n, ranges, True)
                if s % 2 == 0:
                    even += 1
                else:
                    odd += 1
            t = s - 1
            if t >= 0 and role in (0, 2):
                if t % 2 == (0 if role == 0 else 1):
                    events["B"] = (SIDE + side, [(0, even), (4, odd), (SIDE, side), (THIRD, third)], True)
                    side += 1
                if t in (TO_0 if role == 0 else TO_2):
                    events["C"] = (THIRD + third, [(0, even), (4, odd), (SIDE, side)], False)
                    third += 1
            if t >= 0 and role == 1:
                events["B"] = (SIDE + high, [(0, even), (B0, low), (LATE_0, late_low)], False)
                high += 1
                events["C"] = (B0 + low, [(4, odd), (SIDE, high), (LATE_2, late_high)], False)
                low += 1
                if s - 2 in RELAY_0:
                    events["D"] = (LATE_0 + late_low, [(4, odd), (SIDE, high)], False)
                    late_low += 1
                if s - 2 in RELAY_2:
                    events["D"] = (LATE_2 + late_high, [(0, even), (B0, low)], False)
                    late_high += 1
            steps.append(events)
        tables.append(steps)
    return tables


def kernel(emb, ids, order, out, unit, onehot, packed, rows, pos_rows, ord_rows, pos_col, ord_col,
           ord_out, ord_in, ord_lane, ord_sub, row_best, col_best, staged, shares, final, back,
           send_sem, recv_sem, osend_sem, orecv_sem, ysend_sem, yrecv_sem, yosend_sem, yorecv_sem,
           share_send, share_recv, back_send, back_recv):
    owner = lax.axis_index("owner")
    loop = lax.axis_index("loop")
    x, z, core = owner // 8, lax.rem(owner // 2, 4), lax.rem(owner, 2)
    role = jnp.where(core == 0, loop, lax.rem(loop + 2, 4))

    has_role = [(role == r).astype(jnp.int32) for r in range(4)]

    def device_of_role(r):
        return owner, lax.rem(r + 2 * core, 4)

    def by_role(values):
        if all(v == values[0] for v in values):
            return values[0]
        return sum(has_role[r] * values[r] for r in range(4) if values[r])

    def peers(step, sign):
        found = []
        for h, (dx, dz) in enumerate(OFFSETS[step]):
            for dc in range(2):
                slot = 4 * place(step) + 2 * h + dc
                if slot:
                    px = lax.rem(x + (dx if sign > 0 else 4 - dx), 4)
                    pz = lax.rem(z + (dz if sign > 0 else 4 - dz), 4)
                    pc = lax.rem(core + dc, 2)
                    found.append((slot, ((px * 4 + pz) * 2 + pc, loop)))
        return found

    barrier = pltpu.get_barrier_semaphore()
    for step in range(STEPS):
        for _, peer in peers(step, 1):
            pl.semaphore_signal(barrier, 1, device_id=peer, device_id_type=MESH)
    shares[...] = jnp.full(shares.shape, -1.0, jnp.float32)
    for d in (1, 2, 3):
        pl.semaphore_signal(barrier, 1, device_id=(owner, lax.rem(loop + d, 4)), device_id_type=MESH)

    cluster = ids[...]
    dx = (cluster // 8 - x + 4) % 4
    dz = (cluster // 2 % 4 - z + 4) % 4
    dc = (cluster - core + 2) % 2
    chip = dx * 4 + dz
    slot = jnp.zeros_like(cluster)
    for step in range(STEPS):
        for h, (ox, oz) in enumerate(OFFSETS[step]):
            slot = jnp.where(chip == ox * 4 + oz, 4 * place(step) + 2 * h, slot)
    slot = slot + dc
    slot_iota = lax.broadcasted_iota(jnp.int32, (32, 128), 0)
    hits = [(slot_iota == slot[j:j + 1, :]).astype(jnp.float32) for j in range(8)]
    earlier = (lax.broadcasted_iota(jnp.int32, (128, 128), 0)
               < lax.broadcasted_iota(jnp.int32, (128, 128), 1)).astype(jnp.bfloat16)
    before = jnp.zeros((32, 1), jnp.float32)
    for j in range(8):
        prefix = jnp.dot(hits[j].astype(jnp.bfloat16), earlier, preferred_element_type=jnp.float32)
        rank = jnp.sum(hits[j] * (prefix + before), axis=0, keepdims=True)
        before = before + jnp.sum(hits[j], axis=1, keepdims=True)
        pos = slot[j:j + 1, :].astype(jnp.float32) * CAP + rank
        pos_rows[j:j + 1, :] = pos
        pos_col[j * 128:(j + 1) * 128, :] = jnp.broadcast_to(pos, (128, 128)).T
        when = order[j:j + 1, :].astype(jnp.float32) - FAR
        ord_col[j * 128:(j + 1) * 128, :] = jnp.broadcast_to(when, (128, 128)).T

    def normalize(i, _):
        r = pl.ds(pl.multiple_of(i * 128, 128), 128)
        wide = emb[r, :].astype(jnp.float32)
        scale = lax.rsqrt(jnp.sum(wide * wide, axis=-1, keepdims=True) + epsilon)
        unit[r, :] = (wide * scale).astype(jnp.bfloat16)
        return 0

    lax.fori_loop(0, ROWS // 128, normalize, 0)

    def send(half):
        for s, peer in peers(half // 2, 1):
            if s // 2 % 2 != half % 2:
                continue
            data = pltpu.make_async_remote_copy(
                src_ref=packed.at[pl.ds(s * CAP, CAP)], dst_ref=rows.at[pl.ds(s * CAP, CAP)],
                send_sem=send_sem.at[half], recv_sem=recv_sem.at[half], device_id=peer, device_id_type=MESH)
            data.start()
            when = pltpu.make_async_remote_copy(
                src_ref=ord_out.at[s // 2], dst_ref=ord_in.at[s],
                send_sem=osend_sem.at[half], recv_sem=orecv_sem.at[half], device_id=peer, device_id_type=MESH)
            when.start()

    def exchange_wait(half, sem, osem):
        skip = 1 if half == 0 else 0
        first = 4 * place(half // 2) + 2 * (half % 2) + skip
        r = pl.ds(first * CAP, (2 - skip) * CAP)
        pltpu.make_async_copy(packed.at[r], rows.at[r], sem.at[half]).wait()
        o = pl.ds(first, 2 - skip)
        pltpu.make_async_copy(ord_in.at[o], ord_in.at[o], osem.at[half]).wait()

    lane = lax.broadcasted_iota(jnp.int32, (1024, 128), 1).astype(jnp.float32)
    for step in range(STEPS):
        first = place(step) * CHUNK
        wanted = lax.broadcasted_iota(jnp.int32, (CHUNK, 128), 0).astype(jnp.float32) + float(first)
        for j in range(8):
            onehot[:, j * 128:(j + 1) * 128] = (
                wanted == pos_rows[j:j + 1, :]).astype(jnp.float32).astype(jnp.bfloat16)
        block = jnp.dot(onehot[...], unit[...], preferred_element_type=jnp.float32).astype(jnp.bfloat16)
        packed[first:first + CHUNK, :] = block
        for pair in range(first // 128, first // 128 + 2):
            hit = pos_col[...] == lane + float(pair * 128)
            when = jnp.sum(jnp.where(hit, ord_col[...], 0.0), axis=0, keepdims=True) + FAR
            ord_out[pair] = jnp.broadcast_to(when, (8, 128))
        if step == 0:
            rows[0:CAP, :] = block[0:CAP, :]
            ord_in[0] = ord_out[0]
            pl.semaphore_wait(barrier, 34)
        for half in (2 * step, 2 * step + 1):
            if half < WINDOW:
                send(half)

    def clear(i, _):
        row_best[pl.ds(pl.multiple_of(i * CHUNK, CHUNK), CHUNK), :] = jnp.full((CHUNK, 128), -1.0, jnp.float32)
        col_best[pl.ds(2 * i, 2)] = jnp.full((2, 8, 128), -1.0, jnp.float32)
        return 0

    lax.fori_loop(0, CHUNKS, clear, 0)

    def spread(n):
        for h in range(2):
            when = jnp.broadcast_to(ord_lane[2 * n + h][0:1, :], (128, 128))
            at = n * CHUNK + h * 128
            ord_sub[pl.ds(at if isinstance(at, int) else pl.multiple_of(at, 128), 128), :] = when.T

    def rows_of(n):
        at = n * CHUNK
        return pl.ds(at if isinstance(at, int) else pl.multiple_of(at, CHUNK), CHUNK)

    def cross(ms, n):
        held = jnp.concatenate([rows[rows_of(m), :] for m in ms], axis=0)
        s = lax.dot_general(held, rows[rows_of(n), :], (((1,), (1,)), ((), ())), preferred_element_type=jnp.float32)
        for k, m in enumerate(ms):
            mine = ord_sub[rows_of(m), :]
            best = row_best[rows_of(m), :]
            for h in range(2):
                part = s[k * CHUNK:(k + 1) * CHUNK, h * 128:(h + 1) * 128]
                when = ord_lane[2 * n + h][0:1, :]
                best = jnp.maximum(best, jnp.where(when < mine, part, -1.0))
                other = jnp.where(mine < when, part, -1.0).reshape(CHUNK // 8, 8, 128)
                col_best[2 * n + h] = jnp.maximum(col_best[2 * n + h], jnp.max(other, axis=0))
            row_best[rows_of(m), :] = best

    tables = plan()

    def meet(s, name):
        events = [tables[r][s].get(name) for r in range(4)]
        n = by_role([e[0] if e else 0 for e in events])
        lists = [[r for r in e[1] if r[1]] + ([(e[0], 1)] if e[2] else []) if e else [] for e in events]
        depth = max(len(ranges) for ranges in lists)
        if not depth:
            return
        starts, counts = [], []
        for k in range(depth):
            ranges = [ranges[k] if k < len(ranges) else (0, 0) for ranges in lists]
            starts.append(by_role([r[0] for r in ranges]))
            counts.append(by_role([r[1] for r in ranges]))
        totals = [sum(r[1] for r in ranges) for ranges in lists]
        total, group = by_role(totals), width(totals)

        def member(t):
            t = jnp.minimum(t, total - 1)
            m = t + starts[0]
            passed = counts[0]
            for k in range(1, depth):
                m = jnp.where(t >= passed, t - passed + starts[k], m)
                passed = passed + counts[k]
            return m

        def body(t, _):
            cross([member(t * group + k) for k in range(group)], n)
            return 0

        lax.fori_loop(0, (total + group - 1) // group, body, 0)

    def share_rows(src, dst, h, to, send_index):
        recv_index = 2 * (dst - 8) + h
        data = pltpu.make_async_remote_copy(
            src_ref=rows.at[pl.ds(src * CHUNK + h * 128, 128)], dst_ref=rows.at[pl.ds(dst * CHUNK + h * 128, 128)],
            send_sem=ysend_sem.at[send_index], recv_sem=yrecv_sem.at[recv_index],
            device_id=device_of_role(to), device_id_type=MESH)
        when = pltpu.make_async_remote_copy(
            src_ref=ord_lane.at[2 * src + h], dst_ref=ord_lane.at[2 * dst + h],
            send_sem=yosend_sem.at[send_index], recv_sem=yorecv_sem.at[recv_index],
            device_id=device_of_role(to), device_id_type=MESH)
        return data, when

    sends = [[], [], [], []]

    def pass_on(r, src, dst, h, to):
        for copy in share_rows(src, dst, h, to, len(sends[r])):
            copy.start()
        sends[r].append((src, dst, h, to))

    def forward(s, h):
        n = place(s)
        for r in range(4):
            @pl.when(role == r)
            def _():
                if r == 0:
                    pass_on(0, n, B0 + s, h, 1)
                if r == 1:
                    pass_on(1, n, SIDE + s // 2, h, 0 if s % 2 == 0 else 2)
                if r == 2:
                    pass_on(2, n, SIDE + s, h, 1)
                if r == 3 and KEPT[s] in "pq":
                    pass_on(3, n, THIRD + TO_0.index(s), h, 0)
                if r == 3 and KEPT[s] in "pr":
                    pass_on(3, n, THIRD + TO_2.index(s), h, 2)

    def arrive(s, name):
        events = [tables[r][s].get(name) for r in range(4)]
        for r in range(4):
            if not events[r]:
                continue

            @pl.when(role == r)
            def _():
                n = events[r][0]
                relays = {0: RELAY_0, 2: RELAY_2}.get(r, [])
                for h in range(2):
                    for copy in share_rows(n, n, h, (r + 1) % 4, 0):
                        copy.wait_recv()
                    if name == "C" and s - 1 in relays:
                        late = (LATE_0 if r == 0 else LATE_2) + relays.index(s - 1)
                        pass_on(r, n, late, h, 1)
                spread(n)

    low_half = lax.broadcasted_iota(jnp.int32, (8, 128), 1) < CAP
    for s in range(STEPS + 1):
        if s < STEPS:
            n = place(s)
            for h in range(2):
                half = 2 * s + h
                exchange_wait(half, send_sem, osend_sem)
                if half + WINDOW < 2 * STEPS:
                    send(half + WINDOW)
                exchange_wait(half, recv_sem, orecv_sem)
                ord_lane[2 * n + h] = jnp.where(low_half, ord_in[4 * n + 2 * h], ord_in[4 * n + 2 * h + 1])
                forward(s, h)
            spread(n)
            meet(s, "A")
        for names in ("BC", "D"):
            present = [name for name in names if any(tables[r][s].get(name) for r in range(4))]
            for name in present:
                arrive(s, name)
            for name in present:
                meet(s, name)

    def line(i):
        turned = row_best[i * 128:(i + 1) * 128, :].T
        return jnp.maximum(jnp.max(turned, axis=0, keepdims=True), jnp.max(col_best[i], axis=0, keepdims=True))

    def give(r, groups):
        @pl.when(role == r)
        def _():
            copies = []
            for to, pairs in groups:
                used = {place(step): n for n, step in pairs}
                for p in range(STEPS):
                    for h in range(2):
                        i = 2 * p + h
                        value = line(2 * used[p] + h) if p in used else jnp.full((1, 128), -1.0, jnp.float32)
                        staged[to, i // 8, i % 8:i % 8 + 1, :] = value
                copies.append(pltpu.make_async_remote_copy(
                    src_ref=staged.at[to], dst_ref=shares.at[r], send_sem=share_send.at[to],
                    recv_sem=share_recv.at[r], device_id=device_of_role(to), device_id_type=MESH))
                copies[-1].start()

    give(0, [(3, [(THIRD + k, t) for k, t in enumerate(TO_0)]), (1, [(SIDE + k, 2 * k) for k in range(4)])])
    give(2, [(3, [(THIRD + k, t) for k, t in enumerate(TO_2)]), (1, [(SIDE + k, 2 * k + 1) for k in range(4)])])
    late = [(LATE_0 + k, t) for k, t in enumerate(RELAY_0)] + [(LATE_2 + k, t) for k, t in enumerate(RELAY_2)]
    give(1, [(3, late),
             (0, [(B0 + k, k) for k in range(8)]), (2, [(SIDE + k, k) for k in range(8)])])
    for i in range(16):
        final[i] = jnp.broadcast_to(line(i), (8, 128))
    for r, givers in enumerate(((1,), (0, 2), (1,), (0, 1, 2))):
        @pl.when(role == r)
        def _():
            for giver in givers:
                pltpu.make_async_remote_copy(
                    src_ref=staged.at[0], dst_ref=shares.at[giver], send_sem=share_send.at[0],
                    recv_sem=share_recv.at[giver], device_id=device_of_role(giver),
                    device_id_type=MESH).wait_recv()

    for i in range(16):
        value = shares[0, i // 8, i % 8:i % 8 + 1, :]
        for r in range(1, 3):
            value = jnp.maximum(value, shares[r, i // 8, i % 8:i % 8 + 1, :])
        final[i] = jnp.maximum(final[i], value)
    back[0] = final[0]
    for step in FAR_FIRST:
        for s, peer in peers(step, -1):
            pltpu.make_async_remote_copy(
                src_ref=final.at[s // 2], dst_ref=back.at[s], send_sem=back_send.at[0],
                recv_sem=back_recv.at[0], device_id=peer, device_id_type=MESH).start()
    pltpu.make_async_copy(back.at[pl.ds(1, 31)], back.at[pl.ds(1, 31)], back_recv.at[0]).wait()
    for i in range(16):
        final_line = jnp.where(low_half, back[2 * i], back[2 * i + 1])
        ord_in[i] = final_line

    def collect(j, _):
        at = pos_col[pl.ds(pl.multiple_of(j * 128, 128), 128), :]
        found = jnp.zeros((128, 128), jnp.float32)
        spot = lane[0:128, :]
        for i in range(16):
            found = jnp.where(at == spot + float(i * 128), ord_in[i][0:1, :], found)
        out[pl.ds(j, 1), :] = jnp.sum(found.T, axis=0, keepdims=True)
        return 0

    lax.fori_loop(0, 8, collect, 0)
    for r, owners in enumerate(((3, 1), (3, 0, 2), (3, 1))):
        @pl.when(role == r)
        def _():
            for to in owners:
                pltpu.make_async_remote_copy(
                    src_ref=staged.at[to], dst_ref=shares.at[r], send_sem=share_send.at[to],
                    recv_sem=share_recv.at[r], device_id=device_of_role(to), device_id_type=MESH).wait_send()
    pltpu.make_async_copy(back.at[pl.ds(1, 31)], back.at[pl.ds(1, 31)], back_send.at[0]).wait()
    for r in range(4):
        @pl.when(role == r)
        def _():
            for index, (src, dst, h, to) in enumerate(sends[r]):
                for copy in share_rows(src, dst, h, to, index):
                    copy.wait_send()


def on_device(embeddings, cluster_ids, row_order):
    best = pl.pallas_call(
        kernel,
        out_shape=jax.ShapeDtypeStruct((8, 128), jnp.float32),
        in_specs=[pl.BlockSpec(memory_space=pltpu.VMEM)] * 3,
        out_specs=pl.BlockSpec(memory_space=pltpu.VMEM),
        scratch_shapes=[
            pltpu.VMEM((ROWS, D), jnp.bfloat16),
            pltpu.VMEM((CHUNK, ROWS), jnp.bfloat16),
            pltpu.VMEM((STEPS * CHUNK, D), jnp.bfloat16),
            pltpu.VMEM((CHUNKS * CHUNK, D), jnp.bfloat16),
            pltpu.VMEM((8, 128), jnp.float32),
            pltpu.VMEM((8, 128), jnp.float32),
            pltpu.VMEM((ROWS, 128), jnp.float32),
            pltpu.VMEM((ROWS, 128), jnp.float32),
            pltpu.VMEM((16, 8, 128), jnp.float32),
            pltpu.VMEM((32, 8, 128), jnp.float32),
            pltpu.VMEM((2 * CHUNKS, 8, 128), jnp.float32),
            pltpu.VMEM((CHUNKS * CHUNK, 128), jnp.float32),
            pltpu.VMEM((CHUNKS * CHUNK, 128), jnp.float32),
            pltpu.VMEM((2 * CHUNKS, 8, 128), jnp.float32),
            pltpu.VMEM((4, 2, 8, 128), jnp.float32),
            pltpu.VMEM((4, 2, 8, 128), jnp.float32),
            pltpu.VMEM((16, 8, 128), jnp.float32),
            pltpu.VMEM((32, 8, 128), jnp.float32),
            pltpu.SemaphoreType.DMA((2 * STEPS,)),
            pltpu.SemaphoreType.DMA((2 * STEPS,)),
            pltpu.SemaphoreType.DMA((2 * STEPS,)),
            pltpu.SemaphoreType.DMA((2 * STEPS,)),
            pltpu.SemaphoreType.DMA((32,)),
            pltpu.SemaphoreType.DMA((48,)),
            pltpu.SemaphoreType.DMA((32,)),
            pltpu.SemaphoreType.DMA((48,)),
            pltpu.SemaphoreType.DMA((4,)),
            pltpu.SemaphoreType.DMA((4,)),
            pltpu.SemaphoreType.DMA((1,)),
            pltpu.SemaphoreType.DMA((1,)),
        ],
        compiler_params=pltpu.CompilerParams(
            collective_id=0, has_side_effects=True, vmem_limit_bytes=56 * 1024 * 1024),
        name="best_match",
    )(embeddings, cluster_ids.reshape(8, 128), row_order.reshape(8, 128))
    return best.reshape(ROWS)


def solution(mesh):
    return jax.shard_map(
        on_device,
        mesh=mesh,
        in_specs=(P(("owner", "loop"), None), P(("owner", "loop")), P(("owner", "loop"))),
        out_specs=P(("owner", "loop")),
        check_vma=False,
    )
```

```python
import functools

import jax
import jax.numpy as jnp
from jax import lax
from jax.experimental import pallas as pl
from jax.experimental.pallas import tpu as pltpu
from jax.sharding import PartitionSpec as P

MESH = pl.DeviceIdType.MESH
epsilon = 1e-06
D = 768
ROWS = 1024
CAP = 64
CHUNK = 256
STEPS = 8
CHUNKS = 32
FAR = float(2 ** 20)
AHEAD = 3
WINDOW = 3
WIDEST = 8


def width(totals):
    def cost(group):
        return max(-(-total // group) for total in totals) * (2.3 + group)

    return min(range(1, WIDEST + 1), key=cost)


OFFSETS = [
    [(0, 0), (2, 2)], [(1, 0), (3, 0)], [(0, 1), (0, 3)], [(1, 1), (3, 3)],
    [(2, 1), (2, 3)], [(1, 3), (3, 1)], [(1, 2), (3, 2)], [(2, 0), (0, 2)],
]
FAR_FIRST = (0, 4, 6, 3, 5, 7, 1, 2)


def place(step):
    return step // 2 + 4 * (step % 2)


KEPT = ["q", "r", "p", "p", "q", "r", "p", "p"]
RELAY_0 = [step for step in range(STEPS) if KEPT[step] == "q"]
RELAY_2 = [step for step in range(STEPS) if KEPT[step] == "r"]
TO_0 = [step for step in range(STEPS) if KEPT[step] in "pq"]
TO_2 = [step for step in range(STEPS) if KEPT[step] in "pr"]
SIDE, THIRD, LATE_2, B0, LATE_0 = 8, 12, 16, 20, 28


def plan():
    tables = []
    for role in range(4):
        even = odd = 0
        side = third = low = high = late_low = late_high = 0
        steps = []
        for s in range(STEPS + 1):
            events = {}
            if s < STEPS:
                n = place(s)
                if role == 1:
                    if s % 2 == 0:
                        ranges = [(4, odd), (SIDE, high), (LATE_2, late_high)]
                    else:
                        ranges = [(0, even), (B0, low), (LATE_0, late_low)]
                    events["A"] = (n, ranges, False)
                else:
                    ranges = [(0, even), (4, odd)]
                    if role != 3:
                        ranges += [(SIDE, side), (THIRD, third)]
                    events["A"] = (n, ranges, True)
                if s % 2 == 0:
                    even += 1
                else:
                    odd += 1
            t = s - 1
            if t >= 0 and role in (0, 2):
                if t % 2 == (0 if role == 0 else 1):
                    events["B"] = (SIDE + side, [(0, even), (4, odd), (SIDE, side), (THIRD, third)], True)
                    side += 1
                if t in (TO_0 if role == 0 else TO_2):
                    events["C"] = (THIRD + third, [(0, even), (4, odd), (SIDE, side)], False)
                    third += 1
            if t >= 0 and role == 1:
                events["B"] = (SIDE + high, [(0, even), (B0, low), (LATE_0, late_low)], False)
                high += 1
                events["C"] = (B0 + low, [(4, odd), (SIDE, high), (LATE_2, late_high)], False)
                low += 1
                if s - 2 in RELAY_0:
                    events["D"] = (LATE_0 + late_low, [(4, odd), (SIDE, high)], False)
                    late_low += 1
                if s - 2 in RELAY_2:
                    events["D"] = (LATE_2 + late_high, [(0, even), (B0, low)], False)
                    late_high += 1
            steps.append(events)
        tables.append(steps)
    return tables


def kernel(emb, ids, order, out, unit, onehot, packed, rows, pos_rows, ord_rows, pos_col, ord_col,
           ord_out, ord_in, ord_lane, ord_sub, row_best, col_best, staged, shares, final, back,
           send_sem, recv_sem, osend_sem, orecv_sem, ysend_sem, yrecv_sem, yosend_sem, yorecv_sem,
           share_send, share_recv, back_send, back_recv):
    owner = lax.axis_index("owner")
    loop = lax.axis_index("loop")
    x, z, core = owner // 8, lax.rem(owner // 2, 4), lax.rem(owner, 2)
    role = jnp.where(core == 0, loop, lax.rem(loop + 2, 4))

    has_role = [(role == r).astype(jnp.int32) for r in range(4)]

    def device_of_role(r):
        return owner, lax.rem(r + 2 * core, 4)

    def by_role(values):
        if all(v == values[0] for v in values):
            return values[0]
        return sum(has_role[r] * values[r] for r in range(4) if values[r])

    def peers(step, sign):
        found = []
        for h, (dx, dz) in enumerate(OFFSETS[step]):
            for dc in range(2):
                slot = 4 * place(step) + 2 * h + dc
                if slot:
                    px = lax.rem(x + (dx if sign > 0 else 4 - dx), 4)
                    pz = lax.rem(z + (dz if sign > 0 else 4 - dz), 4)
                    pc = lax.rem(core + dc, 2)
                    found.append((slot, ((px * 4 + pz) * 2 + pc, loop)))
        return found

    barrier = pltpu.get_barrier_semaphore()
    for step in range(STEPS):
        for _, peer in peers(step, 1):
            pl.semaphore_signal(barrier, 1, device_id=peer, device_id_type=MESH)
    shares[...] = jnp.full(shares.shape, -1.0, jnp.float32)
    for d in (1, 2, 3):
        pl.semaphore_signal(barrier, 1, device_id=(owner, lax.rem(loop + d, 4)), device_id_type=MESH)

    cluster = ids[...]
    dx = (cluster // 8 - x + 4) % 4
    dz = (cluster // 2 % 4 - z + 4) % 4
    dc = (cluster - core + 2) % 2
    chip = dx * 4 + dz
    slot = jnp.zeros_like(cluster)
    for step in range(STEPS):
        for h, (ox, oz) in enumerate(OFFSETS[step]):
            slot = jnp.where(chip == ox * 4 + oz, 4 * place(step) + 2 * h, slot)
    slot = slot + dc
    slot_iota = lax.broadcasted_iota(jnp.int32, (32, 128), 0)
    hits = [(slot_iota == slot[j:j + 1, :]).astype(jnp.float32) for j in range(8)]
    earlier = (lax.broadcasted_iota(jnp.int32, (128, 128), 0)
               < lax.broadcasted_iota(jnp.int32, (128, 128), 1)).astype(jnp.bfloat16)
    before = jnp.zeros((32, 1), jnp.float32)
    for j in range(8):
        prefix = jnp.dot(hits[j].astype(jnp.bfloat16), earlier, preferred_element_type=jnp.float32)
        rank = jnp.sum(hits[j] * (prefix + before), axis=0, keepdims=True)
        before = before + jnp.sum(hits[j], axis=1, keepdims=True)
        pos = slot[j:j + 1, :].astype(jnp.float32) * CAP + rank
        pos_rows[j:j + 1, :] = pos
        pos_col[j * 128:(j + 1) * 128, :] = jnp.broadcast_to(pos, (128, 128)).T
        when = order[j:j + 1, :].astype(jnp.float32) - FAR
        ord_col[j * 128:(j + 1) * 128, :] = jnp.broadcast_to(when, (128, 128)).T

    def normalize(i, _):
        r = pl.ds(pl.multiple_of(i * 128, 128), 128)
        wide = emb[r, :].astype(jnp.float32)
        scale = lax.rsqrt(jnp.sum(wide * wide, axis=-1, keepdims=True) + epsilon)
        unit[r, :] = (wide * scale).astype(jnp.bfloat16)
        return 0

    lax.fori_loop(0, ROWS // 128, normalize, 0)

    def send(half):
        for s, peer in peers(half // 2, 1):
            if s // 2 % 2 != half % 2:
                continue
            data = pltpu.make_async_remote_copy(
                src_ref=packed.at[pl.ds(s * CAP, CAP)], dst_ref=rows.at[pl.ds(s * CAP, CAP)],
                send_sem=send_sem.at[half], recv_sem=recv_sem.at[half], device_id=peer, device_id_type=MESH)
            data.start()
            when = pltpu.make_async_remote_copy(
                src_ref=ord_out.at[s // 2], dst_ref=ord_in.at[s],
                send_sem=osend_sem.at[half], recv_sem=orecv_sem.at[half], device_id=peer, device_id_type=MESH)
            when.start()

    def exchange_wait(half, sem, osem):
        skip = 1 if half == 0 else 0
        first = 4 * place(half // 2) + 2 * (half % 2) + skip
        r = pl.ds(first * CAP, (2 - skip) * CAP)
        pltpu.make_async_copy(packed.at[r], rows.at[r], sem.at[half]).wait()
        o = pl.ds(first, 2 - skip)
        pltpu.make_async_copy(ord_in.at[o], ord_in.at[o], osem.at[half]).wait()

    lane = lax.broadcasted_iota(jnp.int32, (1024, 128), 1).astype(jnp.float32)

    def pack(step):
        first = place(step) * CHUNK
        wanted = lax.broadcasted_iota(jnp.int32, (CHUNK, 128), 0).astype(jnp.float32) + float(first)
        for j in range(8):
            onehot[:, j * 128:(j + 1) * 128] = (
                wanted == pos_rows[j:j + 1, :]).astype(jnp.float32).astype(jnp.bfloat16)
        block = jnp.dot(onehot[...], unit[...], preferred_element_type=jnp.float32).astype(jnp.bfloat16)
        packed[first:first + CHUNK, :] = block
        for pair in range(first // 128, first // 128 + 2):
            hit = pos_col[...] == lane + float(pair * 128)
            when = jnp.sum(jnp.where(hit, ord_col[...], 0.0), axis=0, keepdims=True) + FAR
            ord_out[pair] = jnp.broadcast_to(when, (8, 128))
        if step == 0:
            rows[0:CAP, :] = block[0:CAP, :]
            ord_in[0] = ord_out[0]

    for step in range(AHEAD):
        pack(step)
        if step == 0:
            pl.semaphore_wait(barrier, 34)
        for half in (2 * step, 2 * step + 1):
            if half < WINDOW:
                send(half)

    def clear(i, _):
        row_best[pl.ds(pl.multiple_of(i * CHUNK, CHUNK), CHUNK), :] = jnp.full((CHUNK, 128), -1.0, jnp.float32)
        col_best[pl.ds(2 * i, 2)] = jnp.full((2, 8, 128), -1.0, jnp.float32)
        return 0

    lax.fori_loop(0, CHUNKS, clear, 0)

    def spread(n):
        for h in range(2):
            when = jnp.broadcast_to(ord_lane[2 * n + h][0:1, :], (128, 128))
            at = n * CHUNK + h * 128
            ord_sub[pl.ds(at if isinstance(at, int) else pl.multiple_of(at, 128), 128), :] = when.T

    def rows_of(n):
        at = n * CHUNK
        return pl.ds(at if isinstance(at, int) else pl.multiple_of(at, CHUNK), CHUNK)

    def cross(ms, n):
        held = jnp.concatenate([rows[rows_of(m), :] for m in ms], axis=0)
        s = lax.dot_general(held, rows[rows_of(n), :], (((1,), (1,)), ((), ())), preferred_element_type=jnp.float32)
        for k, m in enumerate(ms):
            mine = ord_sub[rows_of(m), :]
            best = row_best[rows_of(m), :]
            for h in range(2):
                part = s[k * CHUNK:(k + 1) * CHUNK, h * 128:(h + 1) * 128]
                when = ord_lane[2 * n + h][0:1, :]
                best = jnp.maximum(best, jnp.where(when < mine, part, -1.0))
                other = jnp.where(mine < when, part, -1.0).reshape(CHUNK // 8, 8, 128)
                col_best[2 * n + h] = jnp.maximum(col_best[2 * n + h], jnp.max(other, axis=0))
            row_best[rows_of(m), :] = best

    tables = plan()

    def meet(s, name):
        events = [tables[r][s].get(name) for r in range(4)]
        n = by_role([e[0] if e else 0 for e in events])
        lists = [[r for r in e[1] if r[1]] + ([(e[0], 1)] if e[2] else []) if e else [] for e in events]
        depth = max(len(ranges) for ranges in lists)
        if not depth:
            return
        starts, counts = [], []
        for k in range(depth):
            ranges = [ranges[k] if k < len(ranges) else (0, 0) for ranges in lists]
            starts.append(by_role([r[0] for r in ranges]))
            counts.append(by_role([r[1] for r in ranges]))
        totals = [sum(r[1] for r in ranges) for ranges in lists]
        total, group = by_role(totals), width(totals)

        def member(t):
            t = jnp.minimum(t, total - 1)
            m = t + starts[0]
            passed = counts[0]
            for k in range(1, depth):
                m = jnp.where(t >= passed, t - passed + starts[k], m)
                passed = passed + counts[k]
            return m

        def body(t, _):
            cross([member(t * group + k) for k in range(group)], n)
            return 0

        lax.fori_loop(0, (total + group - 1) // group, body, 0)

    def share_rows(src, dst, h, to, send_index):
        recv_index = 2 * (dst - 8) + h
        data = pltpu.make_async_remote_copy(
            src_ref=rows.at[pl.ds(src * CHUNK + h * 128, 128)], dst_ref=rows.at[pl.ds(dst * CHUNK + h * 128, 128)],
            send_sem=ysend_sem.at[send_index], recv_sem=yrecv_sem.at[recv_index],
            device_id=device_of_role(to), device_id_type=MESH)
        when = pltpu.make_async_remote_copy(
            src_ref=ord_lane.at[2 * src + h], dst_ref=ord_lane.at[2 * dst + h],
            send_sem=yosend_sem.at[send_index], recv_sem=yorecv_sem.at[recv_index],
            device_id=device_of_role(to), device_id_type=MESH)
        return data, when

    sends = [[], [], [], []]

    def pass_on(r, src, dst, h, to):
        for copy in share_rows(src, dst, h, to, len(sends[r])):
            copy.start()
        sends[r].append((src, dst, h, to))

    def forward(s, h):
        n = place(s)
        for r in range(4):
            @pl.when(role == r)
            def _():
                if r == 0:
                    pass_on(0, n, B0 + s, h, 1)
                if r == 1:
                    pass_on(1, n, SIDE + s // 2, h, 0 if s % 2 == 0 else 2)
                if r == 2:
                    pass_on(2, n, SIDE + s, h, 1)
                if r == 3 and KEPT[s] in "pq":
                    pass_on(3, n, THIRD + TO_0.index(s), h, 0)
                if r == 3 and KEPT[s] in "pr":
                    pass_on(3, n, THIRD + TO_2.index(s), h, 2)

    def arrive(s, name):
        events = [tables[r][s].get(name) for r in range(4)]
        for r in range(4):
            if not events[r]:
                continue

            @pl.when(role == r)
            def _():
                n = events[r][0]
                relays = {0: RELAY_0, 2: RELAY_2}.get(r, [])
                for h in range(2):
                    for copy in share_rows(n, n, h, (r + 1) % 4, 0):
                        copy.wait_recv()
                    if name == "C" and s - 1 in relays:
                        late = (LATE_0 if r == 0 else LATE_2) + relays.index(s - 1)
                        pass_on(r, n, late, h, 1)
                spread(n)

    low_half = lax.broadcasted_iota(jnp.int32, (8, 128), 1) < CAP
    for s in range(STEPS + 1):
        if s < STEPS:
            n = place(s)
            for h in range(2):
                half = 2 * s + h
                exchange_wait(half, send_sem, osend_sem)
                if half + WINDOW < 2 * STEPS:
                    send(half + WINDOW)
                exchange_wait(half, recv_sem, orecv_sem)
                ord_lane[2 * n + h] = jnp.where(low_half, ord_in[4 * n + 2 * h], ord_in[4 * n + 2 * h + 1])
                forward(s, h)
            if s + AHEAD < STEPS:
                pack(s + AHEAD)
            spread(n)
            meet(s, "A")
        for names in ("BC", "D"):
            present = [name for name in names if any(tables[r][s].get(name) for r in range(4))]
            for name in present:
                arrive(s, name)
            for name in present:
                meet(s, name)

    def line(i):
        turned = row_best[i * 128:(i + 1) * 128, :].T
        return jnp.maximum(jnp.max(turned, axis=0, keepdims=True), jnp.max(col_best[i], axis=0, keepdims=True))

    def give(r, groups):
        @pl.when(role == r)
        def _():
            copies = []
            for to, pairs in groups:
                used = {place(step): n for n, step in pairs}
                for p in range(STEPS):
                    for h in range(2):
                        i = 2 * p + h
                        value = line(2 * used[p] + h) if p in used else jnp.full((1, 128), -1.0, jnp.float32)
                        staged[to, i // 8, i % 8:i % 8 + 1, :] = value
                copies.append(pltpu.make_async_remote_copy(
                    src_ref=staged.at[to], dst_ref=shares.at[r], send_sem=share_send.at[to],
                    recv_sem=share_recv.at[r], device_id=device_of_role(to), device_id_type=MESH))
                copies[-1].start()

    give(0, [(3, [(THIRD + k, t) for k, t in enumerate(TO_0)]), (1, [(SIDE + k, 2 * k) for k in range(4)])])
    give(2, [(3, [(THIRD + k, t) for k, t in enumerate(TO_2)]), (1, [(SIDE + k, 2 * k + 1) for k in range(4)])])
    late = [(LATE_0 + k, t) for k, t in enumerate(RELAY_0)] + [(LATE_2 + k, t) for k, t in enumerate(RELAY_2)]
    give(1, [(3, late),
             (0, [(B0 + k, k) for k in range(8)]), (2, [(SIDE + k, k) for k in range(8)])])
    for i in range(16):
        final[i] = jnp.broadcast_to(line(i), (8, 128))
    for r, givers in enumerate(((1,), (0, 2), (1,), (0, 1, 2))):
        @pl.when(role == r)
        def _():
            for giver in givers:
                pltpu.make_async_remote_copy(
                    src_ref=staged.at[0], dst_ref=shares.at[giver], send_sem=share_send.at[0],
                    recv_sem=share_recv.at[giver], device_id=device_of_role(giver),
                    device_id_type=MESH).wait_recv()

    for i in range(16):
        value = shares[0, i // 8, i % 8:i % 8 + 1, :]
        for r in range(1, 3):
            value = jnp.maximum(value, shares[r, i // 8, i % 8:i % 8 + 1, :])
        final[i] = jnp.maximum(final[i], value)
    back[0] = final[0]
    for step in FAR_FIRST:
        for s, peer in peers(step, -1):
            pltpu.make_async_remote_copy(
                src_ref=final.at[s // 2], dst_ref=back.at[s], send_sem=back_send.at[0],
                recv_sem=back_recv.at[0], device_id=peer, device_id_type=MESH).start()
    pltpu.make_async_copy(back.at[pl.ds(1, 31)], back.at[pl.ds(1, 31)], back_recv.at[0]).wait()
    for i in range(16):
        final_line = jnp.where(low_half, back[2 * i], back[2 * i + 1])
        ord_in[i] = final_line

    def collect(j, _):
        at = pos_col[pl.ds(pl.multiple_of(j * 128, 128), 128), :]
        found = jnp.zeros((128, 128), jnp.float32)
        spot = lane[0:128, :]
        for i in range(16):
            found = jnp.where(at == spot + float(i * 128), ord_in[i][0:1, :], found)
        out[pl.ds(j, 1), :] = jnp.sum(found.T, axis=0, keepdims=True)
        return 0

    lax.fori_loop(0, 8, collect, 0)
    for r, owners in enumerate(((3, 1), (3, 0, 2), (3, 1))):
        @pl.when(role == r)
        def _():
            for to in owners:
                pltpu.make_async_remote_copy(
                    src_ref=staged.at[to], dst_ref=shares.at[r], send_sem=share_send.at[to],
                    recv_sem=share_recv.at[r], device_id=device_of_role(to), device_id_type=MESH).wait_send()
    pltpu.make_async_copy(back.at[pl.ds(1, 31)], back.at[pl.ds(1, 31)], back_send.at[0]).wait()
    for r in range(4):
        @pl.when(role == r)
        def _():
            for index, (src, dst, h, to) in enumerate(sends[r]):
                for copy in share_rows(src, dst, h, to, index):
                    copy.wait_send()


def on_device(embeddings, cluster_ids, row_order):
    best = pl.pallas_call(
        kernel,
        out_shape=jax.ShapeDtypeStruct((8, 128), jnp.float32),
        in_specs=[pl.BlockSpec(memory_space=pltpu.VMEM)] * 3,
        out_specs=pl.BlockSpec(memory_space=pltpu.VMEM),
        scratch_shapes=[
            pltpu.VMEM((ROWS, D), jnp.bfloat16),
            pltpu.VMEM((CHUNK, ROWS), jnp.bfloat16),
            pltpu.VMEM((STEPS * CHUNK, D), jnp.bfloat16),
            pltpu.VMEM((CHUNKS * CHUNK, D), jnp.bfloat16),
            pltpu.VMEM((8, 128), jnp.float32),
            pltpu.VMEM((8, 128), jnp.float32),
            pltpu.VMEM((ROWS, 128), jnp.float32),
            pltpu.VMEM((ROWS, 128), jnp.float32),
            pltpu.VMEM((16, 8, 128), jnp.float32),
            pltpu.VMEM((32, 8, 128), jnp.float32),
            pltpu.VMEM((2 * CHUNKS, 8, 128), jnp.float32),
            pltpu.VMEM((CHUNKS * CHUNK, 128), jnp.float32),
            pltpu.VMEM((CHUNKS * CHUNK, 128), jnp.float32),
            pltpu.VMEM((2 * CHUNKS, 8, 128), jnp.float32),
            pltpu.VMEM((4, 2, 8, 128), jnp.float32),
            pltpu.VMEM((4, 2, 8, 128), jnp.float32),
            pltpu.VMEM((16, 8, 128), jnp.float32),
            pltpu.VMEM((32, 8, 128), jnp.float32),
            pltpu.SemaphoreType.DMA((2 * STEPS,)),
            pltpu.SemaphoreType.DMA((2 * STEPS,)),
            pltpu.SemaphoreType.DMA((2 * STEPS,)),
            pltpu.SemaphoreType.DMA((2 * STEPS,)),
            pltpu.SemaphoreType.DMA((32,)),
            pltpu.SemaphoreType.DMA((48,)),
            pltpu.SemaphoreType.DMA((32,)),
            pltpu.SemaphoreType.DMA((48,)),
            pltpu.SemaphoreType.DMA((4,)),
            pltpu.SemaphoreType.DMA((4,)),
            pltpu.SemaphoreType.DMA((1,)),
            pltpu.SemaphoreType.DMA((1,)),
        ],
        compiler_params=pltpu.CompilerParams(
            collective_id=0, has_side_effects=True, vmem_limit_bytes=56 * 1024 * 1024),
        name="best_match",
    )(embeddings, cluster_ids.reshape(8, 128), row_order.reshape(8, 128))
    return best.reshape(ROWS)


def solution(mesh):
    return jax.shard_map(
        on_device,
        mesh=mesh,
        in_specs=(P(("owner", "loop"), None), P(("owner", "loop")), P(("owner", "loop"))),
        out_specs=P(("owner", "loop")),
        check_vma=False,
    )
```
